256 devices in a mesh: pool: 32 (over z, y_lo, core), pw: 8 (over x, y_hi).
Axes of the slice: x: 4, y: 4 (y_hi: 2, y_lo: 2; y = y_hi * 2 + y_lo), z: 8, core: 2. Of those that a mesh axis runs over, the one named last changes fastest.
Arguments:
- wave_block: bfloat16 [32, 2, 8, 61440], P('pool', None, None, 'pw'), may hold values from -6 to 6
- occupied: bfloat16 [32, 2, 64, 61440], P('pool', None, None, 'pw'), may hold values from -0.0625 to 0.0625
- radial: bfloat16 [32, 9, 61440], P('pool', None, 'pw'), may hold values from -6 to 6
- k_points: float32 [32, 3], replicated, may hold values from -1 to 1
- g_vectors: float32 [3, 61440], P(None, 'pw'), may hold values from -6 to 6
- structure: bfloat16 [2, 216, 61440], P(None, None, 'pw'), may hold values from -1 to 1, as said below
- positions: float32 [3, 216], replicated, may hold values from 0 to 4
- displacement: float32 [3, 216], replicated, may hold values from -6 to 6
- coupling: float32 [2, 9, 9], replicated, may hold values from -2 to 2
- atom_kind: int32 [216], replicated, may hold values from 0 to 1
- kq_index: int32 [32], replicated, may hold values from 0 to 31, as said below
- occ_count: int32 [32], replicated, may hold values from 32 to 64, as said below
Outputs:
- response: bfloat16 [32, 2, 8, 61440], P('pool', None, None, 'pw')
The draws below stay inside these ranges and needn't reach their ends.
Inputs may be any that keep to these rules, and one draw needn't show every extreme that they name: structure[0] and structure[1] are the cosine and sine of one angle. kq_index[k] = (k + s) mod 32 for one s, the same for every k, where s is a power of two below 32. `occ_count`: some k-point has exactly 64 occupied bands.
All inputs are finite; a program needn't handle non-finite values.
Results may differ from the reference program's by a relative error of at most 0.024.
Values may be sent and summed in bfloat16 or wider, within the bound.
A program may use at most 64 MiB of HBM per device.

```python
import math
import jax
import jax.numpy as jnp
from jax import lax

ATOMS = 216
TYPES = 9
KINDS = 2
PW = 61440
BANDS = 8
OCC_MAX = 64
KPOINTS = 32


def draw_structure(key, part):
    key = jax.random.fold_in(key, 11)
    angles = jax.random.uniform(key, (ATOMS, PW), jnp.float32, -math.pi, math.pi)
    return jnp.stack([jnp.cos(angles), jnp.sin(angles)]).astype(jnp.bfloat16)


def draw_kq_index(key, part):
    key = jax.random.fold_in(key, 12)
    level_count = (KPOINTS - 1).bit_length()
    level_pick = jax.random.randint(key, (), 0, level_count, dtype=jnp.int32)
    offset_amount = jnp.left_shift(jnp.int32(1), level_pick)
    return jnp.mod(jnp.arange(KPOINTS, dtype=jnp.int32) + offset_amount, KPOINTS)


def draw_occ_count(key, part):
    key = jax.random.fold_in(key, 13)
    first_key, second_key = jax.random.split(key)
    counts = jax.random.randint(first_key, (KPOINTS,), OCC_MAX // 2, OCC_MAX + 1, dtype=jnp.int32)
    fullest = jax.random.randint(second_key, (), 0, KPOINTS, dtype=jnp.int32)
    return jnp.where(jnp.arange(KPOINTS, dtype=jnp.int32) == fullest, OCC_MAX, counts)


def with_ends(entries, rng, smallest, top_value):
    shape = entries.shape
    place = [jax.random.randint(jax.random.fold_in(rng, axis), (), 0, shape[axis]) for axis in range(len(shape))]
    entries = entries.at[tuple(place)].set(smallest)
    longest = shape.index(max(shape))
    place[longest] = (place[longest] + 1) % shape[longest]
    return entries.at[tuple(place)].set(top_value)


def block_levels(rng, shape, shards, least, top_value):
    def one(dim, shards_of):
        steps = jax.random.uniform(jax.random.fold_in(jax.random.fold_in(rng, 6), dim), (shards_of,), jnp.float32, least / len(shards), top_value / len(shards))
        return jnp.repeat(jnp.exp(steps), shape[dim] // shards_of).reshape((-1,) + (1,) * (len(shape) - dim - 1))

    factor_of = one(*shards[0])
    for cut in shards[1:]:
        factor_of = factor_of * one(*cut)
    return factor_of


def normal_values(stream_key, shape, scale, most, shards=(), kind=jnp.bfloat16):
    factor_of = block_levels(stream_key, shape, shards, -0.22, 0.18) if shards else 1.0
    values = jax.random.normal(stream_key, shape, jnp.float32) * scale * factor_of
    return jnp.minimum(jnp.maximum(values, -most), most).astype(kind)


def setup_inputs(seed: int = 0) -> dict:
    keys = jax.random.split(jax.random.key(seed), 13)
    return {
        "wave_block": normal_values(keys[0], (KPOINTS, 2, BANDS, PW), 1.0, 6.0, ((0, 32), (3, 8))),
        "occupied": normal_values(keys[1], (KPOINTS, 2, OCC_MAX, PW), (PW // 6) ** -0.5, 0.0625, ((0, 32), (3, 8))),
        "radial": normal_values(keys[2], (KPOINTS, TYPES, PW), 1.0, 6.0, ((0, 32), (2, 8))),
        "k_points": jnp.clip(jax.random.uniform(keys[3], (KPOINTS, 3), jnp.float32, -1.0, 1.0), -1.0, 1.0),
        "g_vectors": normal_values(keys[4], (3, PW), 1.0, 6.0, ((1, 8),), jnp.float32),
        "structure": draw_structure(jax.random.fold_in(keys[12], 71), 0),
        "positions": jnp.clip(jax.random.uniform(keys[6], (3, ATOMS), jnp.float32, 0.0, 4.0), 0.0, 4.0),
        "displacement": normal_values(keys[7], (3, ATOMS), 1.0, 6.0, (), jnp.float32),
        "coupling": normal_values(keys[8], (KINDS, TYPES, TYPES), TYPES ** -0.5, 2.0, (), jnp.float32),
        "atom_kind": with_ends(jax.random.randint(keys[9], (ATOMS,), 0, KINDS), jax.random.fold_in(keys[9], 1), 0, KINDS - 1).astype(jnp.int32),
        "kq_index": draw_kq_index(jax.random.fold_in(keys[12], 71), 0),
        "occ_count": draw_occ_count(jax.random.fold_in(keys[12], 71), 0),
    }


HIGHEST_PRECISION = lax.Precision.HIGHEST

def plane_weights(kpoint, g_vectors):
    shifted = kpoint[:, None] + g_vectors
    return jnp.concatenate([jnp.ones_like(shifted[:1]), shifted], 0)

def moment_table(wave_rows, radial_rows, kpoint, g_vectors):
    weights = plane_weights(kpoint, g_vectors)
    weight_table = weights[:, None, :] * radial_rows.astype(jnp.float32)[None]
    moments = weight_table[None, :, :, None, :] * wave_rows.astype(jnp.float32)[:, None, None, :, :]
    return moments.reshape(-1, moments.shape[-1]).astype(jnp.bfloat16)

def raw_products(struct_rows, moments, atom_count):
    column_count = moments.shape[0] // 2
    product = lax.dot_general(struct_rows, moments, (((1,), (1,)), ((), ())), preferred_element_type=jnp.float32)
    real_real = product[:atom_count, :column_count]
    real_imag = product[:atom_count, column_count:]
    imag_real = product[atom_count:, :column_count]
    imag_imag = product[atom_count:, column_count:]
    return jnp.stack([real_real + imag_imag, real_imag - imag_real])

def atom_phase(kpoint, positions):
    angles = lax.optimization_barrier(jnp.sum(kpoint[:, None] * positions, 0))
    return (jnp.cos(angles), jnp.sin(angles))

def kind_coupling(atom_kind, coupling):
    onehot = (atom_kind[:, None] == jnp.arange(coupling.shape[0], dtype=jnp.int32)[None, :]).astype(jnp.float32)
    return jnp.einsum('ak,kts->ats', onehot, coupling, precision=HIGHEST_PRECISION)

def vertex_weights(raw_sums, cos_part, sine_part, displacement, kind_rows, type_count, band_count):
    scale_factor = 1.0 / math.sqrt(PW)
    atom_count = raw_sums.shape[1]
    coef_re = (cos_part[:, None] * raw_sums[0] - sine_part[:, None] * raw_sums[1]) * scale_factor
    coef_im = (cos_part[:, None] * raw_sums[1] + sine_part[:, None] * raw_sums[0]) * scale_factor
    coef_re = coef_re.reshape(atom_count, 4, type_count, band_count)
    coef_im = coef_im.reshape(atom_count, 4, type_count, band_count)
    moment_sum_re = jnp.einsum('ga,agtb->atb', displacement, coef_re[:, 1:], precision=HIGHEST_PRECISION)
    moment_sum_im = jnp.einsum('ga,agtb->atb', displacement, coef_im[:, 1:], precision=HIGHEST_PRECISION)
    deriv_re = -moment_sum_im
    deriv_im = moment_sum_re
    coupled_re = jnp.einsum('ats,asb->atb', kind_rows, coef_re[:, 0], precision=HIGHEST_PRECISION)
    coupled_im = jnp.einsum('ats,asb->atb', kind_rows, coef_im[:, 0], precision=HIGHEST_PRECISION)
    dcoupled_re = jnp.einsum('ats,asb->atb', kind_rows, deriv_re, precision=HIGHEST_PRECISION)
    dcoupled_im = jnp.einsum('ats,asb->atb', kind_rows, deriv_im, precision=HIGHEST_PRECISION)
    moving_re = displacement.T[:, :, None, None] * coupled_im[:, None]
    moving_im = -displacement.T[:, :, None, None] * coupled_re[:, None]
    vertex_re = jnp.concatenate([dcoupled_re[:, None], moving_re], 1).reshape(atom_count, -1)
    vertex_im = jnp.concatenate([dcoupled_im[:, None], moving_im], 1).reshape(atom_count, -1)
    return jnp.stack([vertex_re, vertex_im])

def phased_vertex(vertex, cos_part, sine_part):
    scale_factor = 1.0 / math.sqrt(4 * TYPES * ATOMS)
    vert_re = (cos_part[:, None] * vertex[0] + sine_part[:, None] * vertex[1]) * scale_factor
    vert_im = (cos_part[:, None] * vertex[1] - sine_part[:, None] * vertex[0]) * scale_factor
    return jnp.stack([vert_re, vert_im]).astype(jnp.bfloat16)

def applied_wave(vertex_q, struct_rows, radial_rows, kpoint, g_vectors, band_count):
    vert_re = vertex_q[0]
    vert_im = vertex_q[1]
    stacked = jnp.concatenate([jnp.concatenate([vert_re, vert_im], 1), jnp.concatenate([-vert_im, vert_re], 1)], 0)
    spread = lax.dot_general(stacked, struct_rows, (((0,), (0,)), ((), ())), preferred_element_type=jnp.float32)
    type_count = radial_rows.shape[0]
    spread = spread.reshape(2, 4, type_count, band_count, spread.shape[-1])
    weight_table = plane_weights(kpoint, g_vectors)[:, None, :] * radial_rows.astype(jnp.float32)[None]
    return lax.optimization_barrier(jnp.sum(spread * weight_table[None, :, :, None, :], axis=(1, 2))).astype(jnp.bfloat16)

def correlation_terms(occupied_rows, applied):
    occ_rows = occupied_rows.shape[1]
    band_count = applied.shape[1]
    plane_count = applied.shape[2]
    product = lax.dot_general(occupied_rows.reshape(2 * occ_rows, plane_count), applied.reshape(2 * band_count, plane_count), (((1,), (1,)), ((), ())), preferred_element_type=jnp.float32)
    real_real = product[:occ_rows, :band_count]
    real_imag = product[:occ_rows, band_count:]
    imag_real = product[occ_rows:, :band_count]
    imag_imag = product[occ_rows:, band_count:]
    return jnp.stack([real_real + imag_imag, real_imag - imag_real])

def projected(correlation, live_count, occupied_rows, applied):
    occ_rows = occupied_rows.shape[1]
    band_count = applied.shape[1]
    plane_count = applied.shape[2]
    live_rows = jnp.arange(occ_rows, dtype=jnp.int32) < live_count
    kept_rows = jnp.where(live_rows[None, :, None], correlation, 0.0).astype(jnp.bfloat16)
    over_re = kept_rows[0]
    over_im = kept_rows[1]
    stacked = jnp.concatenate([jnp.concatenate([over_re, over_im], 1), jnp.concatenate([-over_im, over_re], 1)], 0)
    removed = lax.dot_general(stacked, occupied_rows.reshape(2 * occ_rows, plane_count), (((0,), (0,)), ((), ())), preferred_element_type=jnp.float32)
    return (applied.astype(jnp.float32) - removed.reshape(2, band_count, plane_count)).astype(jnp.bfloat16)

def reference(wave_block, occupied, radial, k_points, g_vectors, structure, positions, displacement, coupling, atom_kind, kq_index, occ_count):
    atom_count = structure.shape[1]
    struct_rows = structure.reshape(2 * atom_count, structure.shape[2])
    kind_rows = kind_coupling(atom_kind, coupling)
    band_count = wave_block.shape[2]
    type_count = radial.shape[1]

    def one_point(point_index):
        target = kq_index[point_index]
        moments = moment_table(wave_block[point_index], radial[point_index], k_points[point_index], g_vectors)
        raw_sums = raw_products(struct_rows, moments, atom_count)
        cos_part, sine_part = atom_phase(k_points[point_index], positions)
        vertex = vertex_weights(raw_sums, cos_part, sine_part, displacement, kind_rows, type_count, band_count)
        next_cos, next_sine = atom_phase(k_points[target], positions)
        vertex_q = phased_vertex(vertex, next_cos, next_sine)
        applied = applied_wave(vertex_q, struct_rows, radial[target], k_points[target], g_vectors, band_count)
        correlation = correlation_terms(occupied[target], applied)
        return projected(correlation, occ_count[target], occupied[target], applied)
    return lax.map(one_point, jnp.arange(k_points.shape[0], dtype=jnp.int32))
```

```python
import functools
import math

import jax
import jax.numpy as jnp
from jax import lax
from jax.experimental import pallas as pl
from jax.experimental.pallas import tpu as pltpu
from jax.sharding import PartitionSpec as P

ATOMS = 216
TYPES = 9
PW = 61440
GROUP = 4
GROUPS = 2
ROWS = 4 * TYPES
PAD = 40
HALF = 128
MESH = pl.DeviceIdType.MESH
F32 = jnp.float32
BF16 = jnp.bfloat16


def dot_nt(a, b):
    return lax.dot_general(a, b, (((1,), (1,)), ((), ())), preferred_element_type=F32)


def dot_nn(a, b):
    return lax.dot_general(a, b, (((1,), (0,)), ((), ())), preferred_element_type=F32)


def kernel(
    shift,
    wave_in,
    occ_in,
    radial_in,
    kpts_in,
    gvec_in,
    struct_in,
    pos_in,
    disp_in,
    coupling_in,
    kind_in,
    count_in,
    out_ref,
    wave,
    occ,
    radial,
    kpts,
    gvec,
    struct,
    pos_raw,
    disp_raw,
    coupling,
    kind_raw,
    count,
    weights,
    moments,
    acc,
    tables,
    kinds,
    couple,
    coef,
    deriv,
    vert,
    vert_full,
    vert_op,
    applied,
    part_send,
    part_recv,
    vert_send,
    gathered,
    corr_send,
    corr_recv,
    resp_send,
    resp_recv,
    load_sem,
    struct_sem,
    part_ssem,
    part_rsem,
    shift_ssem,
    shift_rsem,
    gather_ssem,
    gather_rsem,
    corr_ssem,
    corr_rsem,
    resp_ssem,
    resp_rsem,
):
    pools = lax.axis_size("pool")
    n = lax.axis_size("pw")
    pool = lax.axis_index("pool")
    me = lax.axis_index("pw")
    ahead = lax.rem(pool + shift, pools)
    behind = lax.rem(pool + pools - shift, pools)
    planes = wave.shape[-1]
    chunks = struct_sem.shape[0]
    width = planes // chunks

    halves = (slice(0, HALF), slice(HALF, ATOMS))

    small = []
    pairs = (
        (radial_in.at[0], radial),
        (gvec_in, gvec),
        (kpts_in, kpts),
        (wave_in.at[0], wave),
        (pos_in, pos_raw),
        (disp_in, disp_raw),
        (coupling_in, coupling),
        (kind_in, kind_raw),
        (count_in, count),
    )
    for i, (src, dst) in enumerate(pairs):
        copy = pltpu.make_async_copy(src, dst, load_sem.at[i])
        copy.start()
        small.append(copy)
    struct_copies = []
    for i in range(chunks):
        span = pl.ds(i * width, width)
        copy = pltpu.make_async_copy(
            struct_in.at[:, :, span], struct.at[:, :, span], struct_sem.at[i]
        )
        copy.start()
        struct_copies.append(copy)
    occ_copy = pltpu.make_async_copy(occ_in.at[0], occ, load_sem.at[len(pairs)])
    occ_copy.start()

    barrier = pltpu.get_barrier_semaphore()
    for j in range(1, n):
        pl.semaphore_signal(
            barrier, inc=1, device_id={"pw": lax.rem(me + j, n)}, device_id_type=MESH
        )
    pool_peers = [ahead] if 2 * shift == pools else [ahead, behind]
    for peer in pool_peers:
        pl.semaphore_signal(barrier, inc=1, device_id={"pool": peer}, device_id_type=MESH)

    for copy in small:
        copy.wait()
    half = lax.rem(me, 2)
    lanes = pl.ds(pl.multiple_of(half * HALF, HALF), HALF)
    tables[...] = jnp.zeros_like(tables)
    tables[0:3, 0:ATOMS] = pos_raw[...]
    tables[3:6, 0:ATOMS] = disp_raw[...]
    kinds[...] = jnp.zeros_like(kinds)
    kinds[0:1, 0:ATOMS] = kind_raw[...]
    here = kpts[pl.ds(pool, 1), :]
    there = kpts[pl.ds(ahead, 1), :]

    def phase(point):
        angle = (
            point[:, 0:1] * tables[0:1, lanes]
            + point[:, 1:2] * tables[1:2, lanes]
            + point[:, 2:3] * tables[2:3, lanes]
        )
        return jnp.cos(angle), jnp.sin(angle)

    cos_here, sin_here = phase(here)
    cos_next, sin_next = phase(there)
    disp = [tables[3 + c : 4 + c, lanes] for c in range(3)]
    second = jnp.broadcast_to(kinds[0:1, lanes], (TYPES, HALF)) == 1
    for u in range(TYPES):
        first_col = jnp.broadcast_to(coupling[0][:, u : u + 1], (TYPES, HALF))
        second_col = jnp.broadcast_to(coupling[1][:, u : u + 1], (TYPES, HALF))
        couple[u] = jnp.where(second, second_col, first_col)
    vert[...] = jnp.zeros_like(vert)
    acc[...] = jnp.zeros_like(acc)

    rad = radial[...].astype(F32)
    weights[0:TYPES, :] = rad
    for c in range(3):
        weights[TYPES * (c + 1) : TYPES * (c + 2), :] = rad * (gvec[c : c + 1, :] + here[:, c : c + 1])

    def block(group, span):
        rows = slice(GROUP * group, GROUP * (group + 1))
        return jnp.concatenate(
            [wave[0, :, span].astype(F32)[rows], wave[1, :, span].astype(F32)[rows]], 0
        )

    def fill_moments(group, span):
        held = block(group, span)
        for i in range(ROWS // 2):
            upper = weights[2 * i : 2 * i + 1, span] * held
            lower = weights[2 * i + 1 : 2 * i + 2, span] * held
            moments[16 * i : 16 * i + 16, span] = jnp.concatenate([upper, lower], 0).astype(BF16)

    def send_parts(group):
        for b in range(GROUP):
            for h in range(2):
                re_rows = pl.ds(b, PAD, stride=8)
                im_rows = pl.ds(GROUP + b, PAD, stride=8)
                raw_re = acc[0, h, re_rows, :] + acc[1, h, im_rows, :]
                raw_im = acc[0, h, im_rows, :] - acc[1, h, re_rows, :]
                part_send[group, 2 * b + h] = jnp.concatenate([raw_re, raw_im], 0).astype(BF16)
        sent = []
        for j in range(1, n):
            peer = lax.rem(me + j, n)
            copy = pltpu.make_async_remote_copy(
                src_ref=part_send.at[group, peer],
                dst_ref=part_recv.at[group, j],
                send_sem=part_ssem.at[group, j],
                recv_sem=part_rsem.at[group, j],
                device_id={"pw": peer},
                device_id_type=MESH,
            )
            copy.start()
            sent.append(copy)
        return sent

    def send_vertex(group):
        total = part_send[group, me].astype(F32)
        for j in range(1, n):
            total += part_recv[group, j].astype(F32)
        scale = 1.0 / math.sqrt(PW)
        coef[0] = (cos_here * total[0:PAD] - sin_here * total[PAD:]) * scale
        coef[1] = (cos_here * total[PAD:] + sin_here * total[0:PAD]) * scale

        def moved(part):
            found = None
            for c in range(3):
                term = disp[c] * coef[part, TYPES * (c + 1) : TYPES * (c + 2), :]
                found = term if found is None else found + term
            return found

        deriv[0, 0:TYPES, :] = -moved(1)
        deriv[1, 0:TYPES, :] = moved(0)

        def coupled(source, part):
            found = None
            for u in range(TYPES):
                term = couple[u] * source[part, u : u + 1, :]
                found = term if found is None else found + term
            return found

        zc_re, zc_im = coupled(coef, 0), coupled(coef, 1)
        pieces = [(coupled(deriv, 0), coupled(deriv, 1))]
        pieces += [(disp[c] * zc_im, -disp[c] * zc_re) for c in range(3)]
        shrink = 1.0 / math.sqrt(4 * TYPES * ATOMS)
        for m, (re, im) in enumerate(pieces):
            vert[TYPES * m : TYPES * (m + 1), :] = (cos_next * re + sin_next * im) * shrink
            vert[PAD + TYPES * m : PAD + TYPES * (m + 1), :] = (cos_next * im - sin_next * re) * shrink
        vert_send[group] = vert[...].astype(BF16)
        copy = pltpu.make_async_remote_copy(
            src_ref=vert_send.at[group],
            dst_ref=gathered.at[group, me],
            send_sem=shift_ssem.at[group],
            recv_sem=shift_rsem.at[group],
            device_id={"pool": ahead},
            device_id_type=MESH,
        )
        copy.start()
        return copy

    def pass_vertex(group):
        sent = []
        for j in range(1, n):
            copy = pltpu.make_async_remote_copy(
                src_ref=gathered.at[group, me],
                dst_ref=gathered.at[group, me],
                send_sem=gather_ssem.at[group, j],
                recv_sem=gather_rsem.at[group, j],
                device_id={"pw": lax.rem(me + j, n)},
                device_id_type=MESH,
            )
            copy.start()
            sent.append(copy)
        return sent

    def apply_vertex(group):
        for b in range(GROUP):
            for h in range(2):
                piece = gathered[group, 2 * b + h].astype(F32)
                re_rows = pl.ds(b, PAD, stride=8)
                im_rows = pl.ds(GROUP + b, PAD, stride=8)
                vert_full[0, h, re_rows, :] = piece[0:PAD]
                vert_full[0, h, im_rows, :] = piece[PAD:]
                vert_full[1, h, re_rows, :] = -piece[PAD:]
                vert_full[1, h, im_rows, :] = piece[0:PAD]
        for h, cols in enumerate(halves):
            width_of = cols.stop - cols.start
            vert_op[:, :, cols] = vert_full[:, h, 0 : 8 * ROWS, 0:width_of].astype(BF16)
        spread = dot_nn(vert_op[0], struct[0])
        spread += dot_nn(vert_op[1], struct[1])
        total = None
        for i in range(ROWS):
            term = weights[i : i + 1, :] * spread[8 * i : 8 * i + 8]
            total = term if total is None else total + term
        applied[group] = total.astype(BF16)

    def send_corr(group):
        corr_send[group] = dot_nt(applied[group], occ[...].reshape(-1, planes))
        sent = []
        for j in range(1, n):
            copy = pltpu.make_async_remote_copy(
                src_ref=corr_send.at[group],
                dst_ref=corr_recv.at[group, j],
                send_sem=corr_ssem.at[group, j],
                recv_sem=corr_rsem.at[group, j],
                device_id={"pw": lax.rem(me + j, n)},
                device_id_type=MESH,
            )
            copy.start()
            sent.append(copy)
        return sent

    count_lane = lax.broadcasted_iota(jnp.int32, (1, pools), 1)
    live = jnp.sum(jnp.where(count_lane == pool, count[...], 0), axis=1, keepdims=True)

    def send_response(group):
        total = corr_send[group]
        for j in range(1, n):
            total += corr_recv[group, j]
        occ_rows = total.shape[1] // 2
        row = lax.broadcasted_iota(jnp.int32, total.shape, 0)
        lane = lax.broadcasted_iota(jnp.int32, total.shape, 1)
        swapped = pltpu.roll(pltpu.roll(total, GROUP, 0), occ_rows, 1)
        same = (row >= GROUP) == (lane >= occ_rows)
        combined = jnp.where(same, total + swapped, total - swapped)
        state = jnp.where(lane >= occ_rows, lane - occ_rows, lane)
        kept = jnp.where(state < live, combined, 0.0).astype(BF16)
        parts = resp_ssem.shape[1]
        length = planes // 2 // parts
        sent = []
        for i in range(parts):
            both = []
            for h in range(2):
                span = pl.ds(h * (planes // 2) + i * length, length)
                removed = dot_nn(kept, occ[:, :, span].reshape(2 * occ_rows, length))
                both.append(applied[group, :, span].astype(F32) - removed)
            span = pl.ds(i * length, length)
            resp_send[group, :, span] = jnp.concatenate(both, 0).astype(BF16)
            copy = pltpu.make_async_remote_copy(
                src_ref=resp_send.at[group, :, span],
                dst_ref=resp_recv.at[group, :, span],
                send_sem=resp_ssem.at[group, i],
                recv_sem=resp_rsem.at[group, i],
                device_id={"pool": behind},
                device_id_type=MESH,
            )
            copy.start()
            sent.append(copy)
        return sent

    for i, copy in enumerate(struct_copies):
        span = pl.ds(i * width, width)
        fill_moments(0, span)
        copy.wait()
        for c in range(2):
            product = dot_nt(moments[:, span], struct[c, :, span])
            for h, cols in enumerate(halves):
                acc[c, h, 0 : 8 * ROWS, 0 : cols.stop - cols.start] += product[:, cols]
    pl.semaphore_wait(barrier, n - 1 + len(pool_peers))
    parts = [send_parts(0)]
    fill_moments(1, pl.ds(0, planes))
    for c in range(2):
        product = dot_nt(moments[...], struct[c])
        for h, cols in enumerate(halves):
            acc[c, h, 0 : 8 * ROWS, 0 : cols.stop - cols.start] = product[:, cols]
    parts.append(send_parts(1))

    shifts = []
    for group in range(GROUPS):
        for copy in parts[group]:
            copy.wait_recv()
        shifts.append(send_vertex(group))
    passes = []
    for group in range(GROUPS):
        shifts[group].wait_recv()
        passes.append(pass_vertex(group))
    occ_copy.wait()
    corrs = []
    for group in range(GROUPS):
        for copy in passes[group]:
            copy.wait_recv()
        apply_vertex(group)
        corrs.append(send_corr(group))
    responses = []
    for group in range(GROUPS):
        for copy in corrs[group]:
            copy.wait_recv()
        responses.append(send_response(group))
    for sent in responses:
        for copy in sent:
            copy.wait_recv()
    mid = planes // 2
    for part in range(2):
        rows = slice(GROUP * part, GROUP * (part + 1))
        for h in range(2):
            found = [
                resp_recv[g, :, :].astype(F32)[8 * h : 8 * h + 8][rows] for g in range(GROUPS)
            ]
            out_ref[0, part, :, h * mid : (h + 1) * mid] = jnp.concatenate(found, 0).astype(BF16)
    for sent in parts + passes + corrs + responses + [shifts]:
        for copy in sent:
            copy.wait_send()


def call(shift, n, pools, chunks, resp_parts, operands):
    wave, occ = operands[0], operands[1]
    planes = wave.shape[-1]
    occ_rows = occ.shape[2]
    vmem, dma = pltpu.VMEM, pltpu.SemaphoreType.DMA
    scratch = [
        vmem((2, 8, planes), BF16),
        vmem((2, occ_rows, planes), BF16),
        vmem((TYPES, planes), BF16),
        vmem((pools, 3), F32),
        vmem((3, planes), F32),
        vmem((2, ATOMS, planes), BF16),
        vmem((3, ATOMS), F32),
        vmem((3, ATOMS), F32),
        vmem((2, TYPES, TYPES), F32),
        vmem((1, ATOMS), jnp.int32),
        vmem((1, pools), jnp.int32),
        vmem((PAD, planes), F32),
        vmem((8 * ROWS, planes), BF16),
        vmem((2, 2, 8 * PAD, HALF), F32),
        vmem((8, 2 * HALF), F32),
        vmem((8, 2 * HALF), jnp.int32),
        vmem((TYPES, TYPES, HALF), F32),
        vmem((2, PAD, HALF), F32),
        vmem((2, 16, HALF), F32),
        vmem((2 * PAD, HALF), F32),
        vmem((2, 2, 8 * PAD, HALF), F32),
        vmem((2, 8 * ROWS, ATOMS), BF16),
        vmem((GROUPS, 8, planes), BF16),
        vmem((GROUPS, n, 2 * PAD, HALF), BF16),
        vmem((GROUPS, n, 2 * PAD, HALF), BF16),
        vmem((GROUPS, 2 * PAD, HALF), BF16),
        vmem((GROUPS, n, 2 * PAD, HALF), BF16),
        vmem((GROUPS, 8, 2 * occ_rows), F32),
        vmem((GROUPS, n, 8, 2 * occ_rows), F32),
        vmem((GROUPS, 16, planes // 2), BF16),
        vmem((GROUPS, 16, planes // 2), BF16),
        dma((10,)),
        dma((chunks,)),
        dma((GROUPS, n)),
        dma((GROUPS, n)),
        dma((GROUPS,)),
        dma((GROUPS,)),
        dma((GROUPS, n)),
        dma((GROUPS, n)),
        dma((GROUPS, n)),
        dma((GROUPS, n)),
        dma((GROUPS, resp_parts)),
        dma((GROUPS, resp_parts)),
    ]
    return pl.pallas_call(
        functools.partial(kernel, shift),
        out_shape=jax.ShapeDtypeStruct(wave.shape, BF16),
        in_specs=[pl.BlockSpec(memory_space=pl.ANY)] * len(operands),
        out_specs=pl.BlockSpec(memory_space=pltpu.VMEM),
        scratch_shapes=scratch,
        compiler_params=pltpu.CompilerParams(
            collective_id=shift.bit_length() - 1,
            has_side_effects=True,
            vmem_limit_bytes=56 * 2**20,
        ),
        name=f"perturb_{shift}",
    )(*operands)


CHUNKS = 4
RESP_PARTS = 2


def local(
    wave_block,
    occupied,
    radial,
    k_points,
    g_vectors,
    structure,
    positions,
    displacement,
    coupling,
    atom_kind,
    kq_index,
    occ_count,
):
    pools = lax.axis_size("pool")
    n = lax.axis_size("pw")
    operands = (
        wave_block,
        occupied,
        radial,
        k_points,
        g_vectors,
        structure,
        positions,
        displacement,
        coupling,
        atom_kind[None, :],
        occ_count[None, :],
    )
    shifts = [1 << level for level in range((pools - 1).bit_length())]
    first = kq_index[0]
    branch = sum((first >= shift).astype(jnp.int32) for shift in shifts[1:])
    runs = [
        functools.partial(lambda shift, *ops: call(shift, n, pools, CHUNKS, RESP_PARTS, ops), shift)
        for shift in shifts
    ]
    return lax.switch(branch, runs, *operands)


def solution(mesh):
    return jax.shard_map(
        local,
        mesh=mesh,
        in_specs=(
            P("pool", None, None, "pw"),
            P("pool", None, None, "pw"),
            P("pool", None, "pw"),
            P(),
            P(None, "pw"),
            P(None, None, "pw"),
            P(),
            P(),
            P(),
            P(),
            P(),
            P(),
        ),
        out_specs=P("pool", None, None, "pw"),
        check_vma=False,
    )
```

```python
import functools
import math

import jax
import jax.numpy as jnp
from jax import lax
from jax.experimental import pallas as pl
from jax.experimental.pallas import tpu as pltpu
from jax.sharding import PartitionSpec as P

ATOMS = 216
TYPES = 9
PW = 61440
GROUP = 4
GROUPS = 2
ROWS = 4 * TYPES
PAD = 40
HALF = 128
MESH = pl.DeviceIdType.MESH
F32 = jnp.float32
BF16 = jnp.bfloat16


def dot_nt(a, b):
    return lax.dot_general(a, b, (((1,), (1,)), ((), ())), preferred_element_type=F32)


def dot_nn(a, b):
    return lax.dot_general(a, b, (((1,), (0,)), ((), ())), preferred_element_type=F32)


def kernel(
    wave_in,
    occ_in,
    radial_in,
    kpts_in,
    gvec_in,
    struct_in,
    pos_in,
    disp_in,
    coupling_in,
    kind_in,
    index_in,
    count_in,
    out_ref,
    wave,
    occ,
    radial,
    kpts,
    gvec,
    struct,
    pos_raw,
    disp_raw,
    coupling,
    kind_raw,
    index,
    count,
    weights,
    moments,
    acc,
    tables,
    kinds,
    couple,
    coef,
    deriv,
    vert,
    vert_full,
    vert_op,
    applied,
    part_send,
    part_recv,
    vert_send,
    candidates,
    gathered,
    corr_send,
    corr_recv,
    load_sem,
    struct_sem,
    part_ssem,
    part_rsem,
    shift_ssem,
    shift_rsem,
    gather_ssem,
    gather_rsem,
    corr_ssem,
    corr_rsem,
):
    pools = lax.axis_size("pool")
    n = lax.axis_size("pw")
    pool = lax.axis_index("pool")
    me = lax.axis_index("pw")
    planes = wave.shape[-1]
    levels = shift_rsem.shape[1]
    halves = (slice(0, HALF), slice(HALF, ATOMS))

    def load(pairs, first):
        copies = []
        for i, (src, dst) in enumerate(pairs):
            copy = pltpu.make_async_copy(src, dst, load_sem.at[first + i])
            copy.start()
            copies.append(copy)
        return copies

    early = load(
        (
            (kpts_in, kpts),
            (radial_in.at[0], radial),
            (gvec_in, gvec),
            (wave_in.at[0], wave),
        ),
        0,
    )
    struct_copies = []
    for i, (start, width) in enumerate(struct_spans(planes)):
        span = pl.ds(start, width)
        copy = pltpu.make_async_copy(
            struct_in.at[:, :, span], struct.at[:, :, span], struct_sem.at[i]
        )
        copy.start()
        struct_copies.append((span, copy))
    late = load(
        (
            (pos_in, pos_raw),
            (disp_in, disp_raw),
            (coupling_in, coupling),
            (kind_in, kind_raw),
            (index_in, index),
            (count_in, count),
            (occ_in.at[0], occ),
        ),
        4,
    )

    barrier = pltpu.get_barrier_semaphore()
    for j in range(1, n):
        pl.semaphore_signal(
            barrier, inc=1, device_id={"pw": lax.rem(me + j, n)}, device_id_type=MESH
        )
    offsets = []
    for level in range(levels):
        offsets += [o for o in (1 << level, pools - (1 << level)) if o not in offsets]
    for offset in offsets:
        pl.semaphore_signal(
            barrier, inc=1, device_id={"pool": lax.rem(pool + offset, pools)}, device_id_type=MESH
        )

    for copy in early:
        copy.wait()
    pool_lane = lax.broadcasted_iota(jnp.int32, (1, pools), 1)

    def pick(values, where):
        return jnp.sum(jnp.where(where, values, jnp.zeros_like(values)), axis=1, keepdims=True)

    here = pick(kpts[...], pool_lane == pool)
    rad = radial[...].astype(F32)
    weights[0:TYPES, :] = rad
    for c in range(3):
        weights[TYPES * (c + 1) : TYPES * (c + 2), :] = rad * (gvec[c : c + 1, :] + here[c : c + 1, :])
    acc[...] = jnp.zeros_like(acc)

    def fill_moments(group, span):
        rows = slice(GROUP * group, GROUP * (group + 1))
        held = jnp.concatenate(
            [wave[0, :, span].astype(F32)[rows], wave[1, :, span].astype(F32)[rows]], 0
        )
        for i in range(ROWS // 2):
            upper = weights[2 * i : 2 * i + 1, span] * held
            lower = weights[2 * i + 1 : 2 * i + 2, span] * held
            moments[group, 16 * i : 16 * i + 16, span] = jnp.concatenate([upper, lower], 0).astype(BF16)

    def send_parts(group):
        for b in range(GROUP):
            for h in range(2):
                re_rows = pl.ds(b, PAD, stride=8)
                im_rows = pl.ds(GROUP + b, PAD, stride=8)
                raw_re = acc[0, h, re_rows, :] + acc[1, h, im_rows, :]
                raw_im = acc[0, h, im_rows, :] - acc[1, h, re_rows, :]
                part_send[group, 2 * b + h] = jnp.concatenate([raw_re, raw_im], 0).astype(BF16)
        sent = []
        for j in range(1, n):
            peer = lax.rem(me + j, n)
            copy = pltpu.make_async_remote_copy(
                src_ref=part_send.at[group, peer],
                dst_ref=part_recv.at[group, j],
                send_sem=part_ssem.at[group, j],
                recv_sem=part_rsem.at[group, j],
                device_id={"pw": peer},
                device_id_type=MESH,
            )
            copy.start()
            sent.append(copy)
        return sent

    for span, copy in struct_copies:
        fill_moments(0, span)
        copy.wait()
        for c in range(2):
            product = dot_nt(moments[0, :, span], struct[c, :, span])
            for h, cols in enumerate(halves):
                acc[c, h, 0 : 8 * ROWS, 0 : cols.stop - cols.start] += product[:, cols]
    pl.semaphore_wait(barrier, n - 1 + len(offsets))
    parts = [send_parts(0)]
    fill_moments(1, pl.ds(0, planes))
    for c in range(2):
        product = dot_nt(moments[1], struct[c])
        for h, cols in enumerate(halves):
            acc[c, h, 0 : 8 * ROWS, 0 : cols.stop - cols.start] = product[:, cols]
    parts.append(send_parts(1))

    for copy in late:
        copy.wait()
    half = lax.rem(me, 2)
    lanes = pl.ds(pl.multiple_of(half * HALF, HALF), HALF)
    tables[...] = jnp.zeros_like(tables)
    tables[0:3, 0:ATOMS] = pos_raw[...]
    tables[3:6, 0:ATOMS] = disp_raw[...]
    kinds[...] = jnp.zeros_like(kinds)
    kinds[0:1, 0:ATOMS] = kind_raw[...]
    target = pick(index[...], pool_lane == pool)
    there = pick(kpts[...], pool_lane == target)
    distance = lax.rem(target - pool + pools, pools)

    def phase(point):
        angle = (
            point[0:1, :] * tables[0:1, lanes]
            + point[1:2, :] * tables[1:2, lanes]
            + point[2:3, :] * tables[2:3, lanes]
        )
        return jnp.cos(angle), jnp.sin(angle)

    cos_here, sin_here = phase(here)
    cos_next, sin_next = phase(there)
    disp = [tables[3 + c : 4 + c, lanes] for c in range(3)]
    second = jnp.broadcast_to(kinds[0:1, lanes], (TYPES, HALF)) == 1
    first_table = coupling[:, 0, :]
    second_table = coupling[:, 1, :]
    for u in range(TYPES):
        first_col = jnp.broadcast_to(first_table[:, u : u + 1], (TYPES, HALF))
        second_col = jnp.broadcast_to(second_table[:, u : u + 1], (TYPES, HALF))
        couple[u] = jnp.where(second, second_col, first_col)
    vert[...] = jnp.zeros_like(vert)

    def send_vertex(group):
        total = part_send[group, me].astype(F32)
        for j in range(1, n):
            total += part_recv[group, j].astype(F32)
        scale = 1.0 / math.sqrt(PW)
        coef[0] = (cos_here * total[0:PAD] - sin_here * total[PAD:]) * scale
        coef[1] = (cos_here * total[PAD:] + sin_here * total[0:PAD]) * scale

        def moved(part):
            found = None
            for c in range(3):
                term = disp[c] * coef[part, TYPES * (c + 1) : TYPES * (c + 2), :]
                found = term if found is None else found + term
            return found

        deriv[0, 0:TYPES, :] = -moved(1)
        deriv[1, 0:TYPES, :] = moved(0)

        def coupled(source, part):
            found = None
            for u in range(TYPES):
                term = couple[u] * source[part, u : u + 1, :]
                found = term if found is None else found + term
            return found

        zc_re, zc_im = coupled(coef, 0), coupled(coef, 1)
        pieces = [(coupled(deriv, 0), coupled(deriv, 1))]
        pieces += [(disp[c] * zc_im, -disp[c] * zc_re) for c in range(3)]
        shrink = 1.0 / math.sqrt(4 * TYPES * ATOMS)
        for m, (re, im) in enumerate(pieces):
            vert[TYPES * m : TYPES * (m + 1), :] = (cos_next * re + sin_next * im) * shrink
            vert[PAD + TYPES * m : PAD + TYPES * (m + 1), :] = (cos_next * im - sin_next * re) * shrink
        vert_send[group] = vert[...].astype(BF16)
        sent = []
        for level in range(levels):
            copy = pltpu.make_async_remote_copy(
                src_ref=vert_send.at[group],
                dst_ref=candidates.at[group, level],
                send_sem=shift_ssem.at[group, level],
                recv_sem=shift_rsem.at[group, level],
                device_id={"pool": lax.rem(pool + (1 << level), pools)},
                device_id_type=MESH,
            )
            copy.start()
            sent.append(copy)
        return sent

    def pass_vertex(group):
        chosen = jnp.zeros((2 * PAD, HALF), F32)
        for level in range(levels):
            chosen = jnp.where(
                distance == (1 << level), candidates[group, level].astype(F32), chosen
            )
        gathered[group, me] = chosen.astype(BF16)
        sent = []
        for j in range(1, n):
            copy = pltpu.make_async_remote_copy(
                src_ref=gathered.at[group, me],
                dst_ref=gathered.at[group, me],
                send_sem=gather_ssem.at[group, j],
                recv_sem=gather_rsem.at[group, j],
                device_id={"pw": lax.rem(me + j, n)},
                device_id_type=MESH,
            )
            copy.start()
            sent.append(copy)
        return sent

    def apply_vertex(group):
        for b in range(GROUP):
            for h in range(2):
                piece = gathered[group, 2 * b + h].astype(F32)
                re_rows = pl.ds(b, PAD, stride=8)
                im_rows = pl.ds(GROUP + b, PAD, stride=8)
                vert_full[0, h, re_rows, :] = piece[0:PAD]
                vert_full[0, h, im_rows, :] = piece[PAD:]
                vert_full[1, h, re_rows, :] = -piece[PAD:]
                vert_full[1, h, im_rows, :] = piece[0:PAD]
        for h, cols in enumerate(halves):
            width_of = cols.stop - cols.start
            vert_op[:, :, cols] = vert_full[:, h, 0 : 8 * ROWS, 0:width_of].astype(BF16)
        spread = dot_nn(vert_op[0], struct[0])
        spread += dot_nn(vert_op[1], struct[1])
        total = None
        for i in range(ROWS):
            term = weights[i : i + 1, :] * spread[8 * i : 8 * i + 8]
            total = term if total is None else total + term
        rounded = total.astype(BF16).astype(F32)
        applied[GROUP * group : GROUP * (group + 1), :] = rounded[0:GROUP]
        applied[8 + GROUP * group : 8 + GROUP * (group + 1), :] = rounded[GROUP:]

    shifts = []
    for group in range(GROUPS):
        for copy in parts[group]:
            copy.wait_recv()
        shifts.append(send_vertex(group))
    passes = []
    for group in range(GROUPS):
        for copy in shifts[group]:
            copy.wait_recv()
        passes.append(pass_vertex(group))
    for group in range(GROUPS):
        for copy in passes[group]:
            copy.wait_recv()
        apply_vertex(group)

    occ_rows = occ.shape[1]
    corr_send[...] = dot_nt(applied[...].astype(BF16), occ[...].reshape(2 * occ_rows, planes))
    corrs = []
    for j in range(1, n):
        copy = pltpu.make_async_remote_copy(
            src_ref=corr_send,
            dst_ref=corr_recv.at[j],
            send_sem=corr_ssem.at[j],
            recv_sem=corr_rsem.at[j],
            device_id={"pw": lax.rem(me + j, n)},
            device_id_type=MESH,
        )
        copy.start()
        corrs.append(copy)
    live = pick(count[...], pool_lane == pool)
    for copy in corrs:
        copy.wait_recv()
    total = corr_send[...]
    for j in range(1, n):
        total += corr_recv[j]
    row = lax.broadcasted_iota(jnp.int32, total.shape, 0)
    lane = lax.broadcasted_iota(jnp.int32, total.shape, 1)
    swapped = pltpu.roll(jnp.concatenate([total[8:], total[:8]], 0), occ_rows, 1)
    same = (row >= 8) == (lane >= occ_rows)
    combined = jnp.where(same, total + swapped, total - swapped)
    state = jnp.where(lane >= occ_rows, lane - occ_rows, lane)
    kept = jnp.where(state < live, combined, 0.0).astype(BF16)
    removed = dot_nn(kept, occ[...].reshape(2 * occ_rows, planes))
    response = (applied[...] - removed).astype(BF16)
    out_ref[0, 0] = response[:8]
    out_ref[0, 1] = response[8:]
    for sent in parts + shifts + passes + [corrs]:
        for copy in sent:
            copy.wait_send()


def struct_spans(planes):
    unit = planes // 20
    return ((0, 4 * unit), (4 * unit, 6 * unit), (10 * unit, 10 * unit))


def perturb(operands, pools, n):
    wave, occ = operands[0], operands[1]
    planes = wave.shape[-1]
    occ_rows = occ.shape[2]
    levels = (pools - 1).bit_length()
    vmem, dma = pltpu.VMEM, pltpu.SemaphoreType.DMA
    scratch = [
        vmem((2, 8, planes), BF16),
        vmem((2, occ_rows, planes), BF16),
        vmem((TYPES, planes), BF16),
        vmem((3, pools), F32),
        vmem((3, planes), F32),
        vmem((2, ATOMS, planes), BF16),
        vmem((3, ATOMS), F32),
        vmem((3, ATOMS), F32),
        vmem((TYPES, 2, TYPES), F32),
        vmem((1, ATOMS), jnp.int32),
        vmem((1, pools), jnp.int32),
        vmem((1, pools), jnp.int32),
        vmem((PAD, planes), F32),
        vmem((GROUPS, 8 * ROWS, planes), BF16),
        vmem((2, 2, 8 * PAD, HALF), F32),
        vmem((8, 2 * HALF), F32),
        vmem((8, 2 * HALF), jnp.int32),
        vmem((TYPES, TYPES, HALF), F32),
        vmem((2, PAD, HALF), F32),
        vmem((2, 16, HALF), F32),
        vmem((2 * PAD, HALF), F32),
        vmem((2, 2, 8 * PAD, HALF), F32),
        vmem((2, 8 * ROWS, ATOMS), BF16),
        vmem((16, planes), F32),
        vmem((GROUPS, n, 2 * PAD, HALF), BF16),
        vmem((GROUPS, n, 2 * PAD, HALF), BF16),
        vmem((GROUPS, 2 * PAD, HALF), BF16),
        vmem((GROUPS, levels, 2 * PAD, HALF), BF16),
        vmem((GROUPS, n, 2 * PAD, HALF), BF16),
        vmem((16, 2 * occ_rows), F32),
        vmem((n, 16, 2 * occ_rows), F32),
        dma((11,)),
        dma((len(struct_spans(planes)),)),
        dma((GROUPS, n)),
        dma((GROUPS, n)),
        dma((GROUPS, levels)),
        dma((GROUPS, levels)),
        dma((GROUPS, n)),
        dma((GROUPS, n)),
        dma((n,)),
        dma((n,)),
    ]
    return pl.pallas_call(
        kernel,
        out_shape=jax.ShapeDtypeStruct(wave.shape, BF16),
        in_specs=[pl.BlockSpec(memory_space=pl.ANY)] * len(operands),
        out_specs=pl.BlockSpec(memory_space=pltpu.VMEM),
        scratch_shapes=scratch,
        compiler_params=pltpu.CompilerParams(
            collective_id=0, has_side_effects=True, vmem_limit_bytes=56 * 2**20
        ),
        name="perturb",
    )(*operands)


def return_kernel(shift, block, out_ref, send_sem, recv_sem):
    pools = lax.axis_size("pool")
    pool = lax.axis_index("pool")
    ahead = lax.rem(pool + shift, pools)
    behind = lax.rem(pool + pools - shift, pools)
    peers = [ahead] if 2 * shift == pools else [ahead, behind]
    barrier = pltpu.get_barrier_semaphore()
    for peer in peers:
        pl.semaphore_signal(barrier, inc=1, device_id={"pool": peer}, device_id_type=MESH)
    pl.semaphore_wait(barrier, len(peers))
    parts = send_sem.shape[0]
    width = block.shape[-1] // parts
    sent = []
    for i in range(parts):
        span = pl.ds(i * width, width)
        copy = pltpu.make_async_remote_copy(
            src_ref=block.at[:, :, :, span],
            dst_ref=out_ref.at[:, :, :, span],
            send_sem=send_sem.at[i],
            recv_sem=recv_sem.at[i],
            device_id={"pool": behind},
            device_id_type=MESH,
        )
        copy.start()
        sent.append(copy)
    for copy in sent:
        copy.wait()


def give_back(shift, parts, block):
    dma = pltpu.SemaphoreType.DMA
    return pl.pallas_call(
        functools.partial(return_kernel, shift),
        out_shape=jax.ShapeDtypeStruct(block.shape, block.dtype),
        in_specs=[pl.BlockSpec(memory_space=pl.ANY)],
        out_specs=pl.BlockSpec(memory_space=pl.ANY),
        scratch_shapes=[dma((parts,)), dma((parts,))],
        compiler_params=pltpu.CompilerParams(
            collective_id=shift.bit_length(), has_side_effects=True
        ),
        name=f"give_back_{shift}",
    )(block)


RETURN_PARTS = 4


def local(
    wave_block,
    occupied,
    radial,
    k_points,
    g_vectors,
    structure,
    positions,
    displacement,
    coupling,
    atom_kind,
    kq_index,
    occ_count,
):
    pools = lax.axis_size("pool")
    n = lax.axis_size("pw")
    operands = (
        wave_block,
        occupied,
        radial,
        k_points.T,
        g_vectors,
        structure,
        positions,
        displacement,
        coupling.transpose(1, 0, 2),
        atom_kind[None, :],
        kq_index[None, :],
        occ_count[None, :],
    )
    block = perturb(operands, pools, n)
    shifts = [1 << level for level in range((pools - 1).bit_length())]
    branch = 31 - lax.clz(kq_index[0])
    runs = [functools.partial(give_back, shift, RETURN_PARTS) for shift in shifts]
    return lax.switch(branch, runs, block)


def solution(mesh):
    return jax.shard_map(
        local,
        mesh=mesh,
        in_specs=(
            P("pool", None, None, "pw"),
            P("pool", None, None, "pw"),
            P("pool", None, "pw"),
            P(),
            P(None, "pw"),
            P(None, None, "pw"),
            P(),
            P(),
            P(),
            P(),
            P(),
            P(),
        ),
        out_specs=P("pool", None, None, "pw"),
        check_vma=False,
    )
```

```python
import functools
import math

import jax
import jax.numpy as jnp
from jax import lax
from jax.experimental import pallas as pl
from jax.experimental.pallas import tpu as pltpu
from jax.sharding import PartitionSpec as P

ATOMS = 216
TYPES = 9
PW = 61440
GROUP = 4
GROUPS = 2
ROWS = 4 * TYPES
PAD = 40
HALF = 128
MESH = pl.DeviceIdType.MESH
F32 = jnp.float32
BF16 = jnp.bfloat16


NEAR = ((2, 1), (1, 1), (3, 1), (2, 0), (0, 1), (1, 0), (3, 0))


def pw_peer(me, n, step, flip):
    return lax.rem(me // 2 + step, n // 2) * 2 + (me % 2 + flip) % 2


def dot_nt(a, b):
    return lax.dot_general(a, b, (((1,), (1,)), ((), ())), preferred_element_type=F32)


def dot_nn(a, b):
    return lax.dot_general(a, b, (((1,), (0,)), ((), ())), preferred_element_type=F32)


def kernel(
    wave_in,
    occ_in,
    radial_in,
    kpts_in,
    gvec_in,
    struct_in,
    pos_in,
    disp_in,
    coupling_in,
    kind_in,
    index_in,
    count_in,
    out_ref,
    wave,
    occ,
    radial,
    kpts,
    gvec,
    struct,
    pos_raw,
    disp_raw,
    coupling,
    kind_raw,
    index,
    count,
    weights,
    moments,
    acc,
    tables,
    kinds,
    couple,
    coef,
    deriv,
    vert,
    vert_full,
    vert_op,
    applied,
    part_send,
    part_recv,
    vert_send,
    candidates,
    gathered,
    corr_send,
    corr_recv,
    load_sem,
    struct_sem,
    part_ssem,
    part_rsem,
    shift_ssem,
    shift_rsem,
    gather_ssem,
    gather_rsem,
    corr_ssem,
    corr_rsem,
):
    pools = lax.axis_size("pool")
    n = lax.axis_size("pw")
    pool = lax.axis_index("pool")
    me = lax.axis_index("pw")
    planes = wave.shape[-1]
    levels = shift_rsem.shape[1]
    halves = (slice(0, HALF), slice(HALF, ATOMS))

    def load(pairs, first):
        copies = []
        for i, (src, dst) in enumerate(pairs):
            copy = pltpu.make_async_copy(src, dst, load_sem.at[first + i])
            copy.start()
            copies.append(copy)
        return copies

    early = load(
        (
            (kpts_in, kpts),
            (radial_in.at[0], radial),
            (gvec_in, gvec),
            (wave_in.at[0], wave),
        ),
        0,
    )
    struct_copies = []
    for i, (start, width) in enumerate(struct_spans(planes)):
        span = pl.ds(start, width)
        copy = pltpu.make_async_copy(
            struct_in.at[:, :, span], struct.at[:, :, span], struct_sem.at[i]
        )
        copy.start()
        struct_copies.append((span, copy))
    late = load(
        (
            (pos_in, pos_raw),
            (disp_in, disp_raw),
            (coupling_in, coupling),
            (kind_in, kind_raw),
            (index_in, index),
            (count_in, count),
            (occ_in.at[0], occ),
        ),
        4,
    )

    barrier = pltpu.get_barrier_semaphore()
    for step, flip in NEAR:
        pl.semaphore_signal(
            barrier, inc=1, device_id={"pw": pw_peer(me, n, step, flip)}, device_id_type=MESH
        )
    for level in reversed(range(levels)):
        sender = lax.rem(pool + pools - (1 << level), pools)
        pl.semaphore_signal(barrier, inc=1, device_id={"pool": sender}, device_id_type=MESH)

    for copy in early:
        copy.wait()
    pool_lane = lax.broadcasted_iota(jnp.int32, (1, pools), 1)

    def pick(values, where):
        return jnp.sum(jnp.where(where, values, jnp.zeros_like(values)), axis=1, keepdims=True)

    here = pick(kpts[...], pool_lane == pool)
    rad = radial[...].astype(F32)
    weights[0:TYPES, :] = rad
    for c in range(3):
        weights[TYPES * (c + 1) : TYPES * (c + 2), :] = rad * (gvec[c : c + 1, :] + here[c : c + 1, :])
    acc[...] = jnp.zeros_like(acc)

    def fill_moments(group, span):
        rows = slice(GROUP * group, GROUP * (group + 1))
        held = jnp.concatenate(
            [wave[0, :, span].astype(F32)[rows], wave[1, :, span].astype(F32)[rows]], 0
        )
        for i in range(ROWS // 2):
            upper = weights[2 * i : 2 * i + 1, span] * held
            lower = weights[2 * i + 1 : 2 * i + 2, span] * held
            moments[group, 16 * i : 16 * i + 16, span] = jnp.concatenate([upper, lower], 0).astype(BF16)

    def send_parts(group):
        for b in range(GROUP):
            for h in range(2):
                re_rows = pl.ds(b, PAD, stride=8)
                im_rows = pl.ds(GROUP + b, PAD, stride=8)
                raw_re = acc[0, h, re_rows, :] + acc[1, h, im_rows, :]
                raw_im = acc[0, h, im_rows, :] - acc[1, h, re_rows, :]
                part_send[group, 2 * b + h] = jnp.concatenate([raw_re, raw_im], 0).astype(BF16)
        sent = []
        for j, (step, flip) in enumerate(NEAR, 1):
            peer = pw_peer(me, n, step, flip)
            copy = pltpu.make_async_remote_copy(
                src_ref=part_send.at[group, peer],
                dst_ref=part_recv.at[group, j],
                send_sem=part_ssem.at[group, j],
                recv_sem=part_rsem.at[group, j],
                device_id={"pw": peer},
                device_id_type=MESH,
            )
            copy.start()
            sent.append(copy)
        return sent

    for span, copy in struct_copies:
        fill_moments(0, span)
        copy.wait()
        for c in range(2):
            product = dot_nt(moments[0, :, span], struct[c, :, span])
            for h, cols in enumerate(halves):
                acc[c, h, 0 : 8 * ROWS, 0 : cols.stop - cols.start] += product[:, cols]
    pl.semaphore_wait(barrier, n - 1 + levels)
    parts = [send_parts(0)]
    fill_moments(1, pl.ds(0, planes))
    for c in range(2):
        product = dot_nt(moments[1], struct[c])
        for h, cols in enumerate(halves):
            acc[c, h, 0 : 8 * ROWS, 0 : cols.stop - cols.start] = product[:, cols]
    parts.append(send_parts(1))

    for copy in late:
        copy.wait()
    half = lax.rem(me, 2)
    lanes = pl.ds(pl.multiple_of(half * HALF, HALF), HALF)
    tables[...] = jnp.zeros_like(tables)
    tables[0:3, 0:ATOMS] = pos_raw[...]
    tables[3:6, 0:ATOMS] = disp_raw[...]
    kinds[...] = jnp.zeros_like(kinds)
    kinds[0:1, 0:ATOMS] = kind_raw[...]
    target = pick(index[...], pool_lane == pool)
    there = pick(kpts[...], pool_lane == target)
    distance = lax.rem(target - pool + pools, pools)

    def phase(point):
        angle = (
            point[0:1, :] * tables[0:1, lanes]
            + point[1:2, :] * tables[1:2, lanes]
            + point[2:3, :] * tables[2:3, lanes]
        )
        return jnp.cos(angle), jnp.sin(angle)

    cos_here, sin_here = phase(here)
    cos_next, sin_next = phase(there)
    disp = [tables[3 + c : 4 + c, lanes] for c in range(3)]
    second = jnp.broadcast_to(kinds[0:1, lanes], (TYPES, HALF)) == 1
    first_table = coupling[:, 0, :]
    second_table = coupling[:, 1, :]
    for u in range(TYPES):
        first_col = jnp.broadcast_to(first_table[:, u : u + 1], (TYPES, HALF))
        second_col = jnp.broadcast_to(second_table[:, u : u + 1], (TYPES, HALF))
        couple[u] = jnp.where(second, second_col, first_col)
    vert[...] = jnp.zeros_like(vert)

    def send_vertex(group):
        total = part_send[group, me].astype(F32)
        for j in range(1, n):
            total += part_recv[group, j].astype(F32)
        scale = 1.0 / math.sqrt(PW)
        coef[0] = (cos_here * total[0:PAD] - sin_here * total[PAD:]) * scale
        coef[1] = (cos_here * total[PAD:] + sin_here * total[0:PAD]) * scale

        def moved(part):
            found = None
            for c in range(3):
                term = disp[c] * coef[part, TYPES * (c + 1) : TYPES * (c + 2), :]
                found = term if found is None else found + term
            return found

        deriv[0, 0:TYPES, :] = -moved(1)
        deriv[1, 0:TYPES, :] = moved(0)

        def coupled(source, part):
            found = None
            for u in range(TYPES):
                term = couple[u] * source[part, u : u + 1, :]
                found = term if found is None else found + term
            return found

        zc_re, zc_im = coupled(coef, 0), coupled(coef, 1)
        pieces = [(coupled(deriv, 0), coupled(deriv, 1))]
        pieces += [(disp[c] * zc_im, -disp[c] * zc_re) for c in range(3)]
        shrink = 1.0 / math.sqrt(4 * TYPES * ATOMS)
        for m, (re, im) in enumerate(pieces):
            vert[TYPES * m : TYPES * (m + 1), :] = (cos_next * re + sin_next * im) * shrink
            vert[PAD + TYPES * m : PAD + TYPES * (m + 1), :] = (cos_next * im - sin_next * re) * shrink
        vert_send[group] = vert[...].astype(BF16)
        sent = []
        for level in reversed(range(levels)):
            copy = pltpu.make_async_remote_copy(
                src_ref=vert_send.at[group],
                dst_ref=candidates.at[group, level],
                send_sem=shift_ssem.at[group, level],
                recv_sem=shift_rsem.at[group, level],
                device_id={"pool": lax.rem(pool + (1 << level), pools)},
                device_id_type=MESH,
            )
            copy.start()
            sent.append(copy)
        return sent

    def pass_vertex(group):
        chosen = jnp.zeros((2 * PAD, HALF), F32)
        for level in range(levels):
            chosen = jnp.where(
                distance == (1 << level), candidates[group, level].astype(F32), chosen
            )
        gathered[group, me] = chosen.astype(BF16)
        sent = []
        for j, (step, flip) in enumerate(NEAR, 1):
            copy = pltpu.make_async_remote_copy(
                src_ref=gathered.at[group, me],
                dst_ref=gathered.at[group, me],
                send_sem=gather_ssem.at[group, j],
                recv_sem=gather_rsem.at[group, j],
                device_id={"pw": pw_peer(me, n, step, flip)},
                device_id_type=MESH,
            )
            copy.start()
            sent.append(copy)
        return sent

    def apply_vertex(group):
        for b in range(GROUP):
            for h in range(2):
                piece = gathered[group, 2 * b + h].astype(F32)
                re_rows = pl.ds(b, PAD, stride=8)
                im_rows = pl.ds(GROUP + b, PAD, stride=8)
                vert_full[0, h, re_rows, :] = piece[0:PAD]
                vert_full[0, h, im_rows, :] = piece[PAD:]
                vert_full[1, h, re_rows, :] = -piece[PAD:]
                vert_full[1, h, im_rows, :] = piece[0:PAD]
        for h, cols in enumerate(halves):
            width_of = cols.stop - cols.start
            vert_op[:, :, cols] = vert_full[:, h, 0 : 8 * ROWS, 0:width_of].astype(BF16)
        spread = dot_nn(vert_op[0], struct[0])
        spread += dot_nn(vert_op[1], struct[1])
        total = None
        for i in range(ROWS):
            term = weights[i : i + 1, :] * spread[8 * i : 8 * i + 8]
            total = term if total is None else total + term
        rounded = total.astype(BF16).astype(F32)
        applied[GROUP * group : GROUP * (group + 1), :] = rounded[0:GROUP]
        applied[8 + GROUP * group : 8 + GROUP * (group + 1), :] = rounded[GROUP:]

    shifts = []
    for group in range(GROUPS):
        for copy in parts[group]:
            copy.wait_recv()
        shifts.append(send_vertex(group))
    passes = []
    for group in range(GROUPS):
        for copy in shifts[group]:
            copy.wait_recv()
        passes.append(pass_vertex(group))
    for group in range(GROUPS):
        for copy in passes[group]:
            copy.wait_recv()
        apply_vertex(group)

    occ_rows = occ.shape[1]
    corr_send[...] = dot_nt(applied[...].astype(BF16), occ[...].reshape(2 * occ_rows, planes))
    corrs = []
    for j, (step, flip) in enumerate(NEAR, 1):
        copy = pltpu.make_async_remote_copy(
            src_ref=corr_send,
            dst_ref=corr_recv.at[j],
            send_sem=corr_ssem.at[j],
            recv_sem=corr_rsem.at[j],
            device_id={"pw": pw_peer(me, n, step, flip)},
            device_id_type=MESH,
        )
        copy.start()
        corrs.append(copy)
    live = pick(count[...], pool_lane == pool)
    for copy in corrs:
        copy.wait_recv()
    total = corr_send[...]
    for j in range(1, n):
        total += corr_recv[j]
    row = lax.broadcasted_iota(jnp.int32, total.shape, 0)
    lane = lax.broadcasted_iota(jnp.int32, total.shape, 1)
    swapped = pltpu.roll(jnp.concatenate([total[8:], total[:8]], 0), occ_rows, 1)
    same = (row >= 8) == (lane >= occ_rows)
    combined = jnp.where(same, total + swapped, total - swapped)
    state = jnp.where(lane >= occ_rows, lane - occ_rows, lane)
    kept = jnp.where(state < live, combined, 0.0).astype(BF16)
    removed = dot_nn(kept, occ[...].reshape(2 * occ_rows, planes))
    response = (applied[...] - removed).astype(BF16)
    out_ref[0, 0] = response[:8]
    out_ref[0, 1] = response[8:]
    for sent in parts + shifts + passes + [corrs]:
        for copy in sent:
            copy.wait_send()


def struct_spans(planes):
    unit = planes // 20
    return ((0, 4 * unit), (4 * unit, 6 * unit), (10 * unit, 10 * unit))


def perturb(operands, pools, n):
    wave, occ = operands[0], operands[1]
    planes = wave.shape[-1]
    occ_rows = occ.shape[2]
    levels = (pools - 1).bit_length()
    vmem, dma = pltpu.VMEM, pltpu.SemaphoreType.DMA
    scratch = [
        vmem((2, 8, planes), BF16),
        vmem((2, occ_rows, planes), BF16),
        vmem((TYPES, planes), BF16),
        vmem((3, pools), F32),
        vmem((3, planes), F32),
        vmem((2, ATOMS, planes), BF16),
        vmem((3, ATOMS), F32),
        vmem((3, ATOMS), F32),
        vmem((TYPES, 2, TYPES), F32),
        vmem((1, ATOMS), jnp.int32),
        vmem((1, pools), jnp.int32),
        vmem((1, pools), jnp.int32),
        vmem((PAD, planes), F32),
        vmem((GROUPS, 8 * ROWS, planes), BF16),
        vmem((2, 2, 8 * PAD, HALF), F32),
        vmem((8, 2 * HALF), F32),
        vmem((8, 2 * HALF), jnp.int32),
        vmem((TYPES, TYPES, HALF), F32),
        vmem((2, PAD, HALF), F32),
        vmem((2, 16, HALF), F32),
        vmem((2 * PAD, HALF), F32),
        vmem((2, 2, 8 * PAD, HALF), F32),
        vmem((2, 8 * ROWS, ATOMS), BF16),
        vmem((16, planes), F32),
        vmem((GROUPS, n, 2 * PAD, HALF), BF16),
        vmem((GROUPS, n, 2 * PAD, HALF), BF16),
        vmem((GROUPS, 2 * PAD, HALF), BF16),
        vmem((GROUPS, levels, 2 * PAD, HALF), BF16),
        vmem((GROUPS, n, 2 * PAD, HALF), BF16),
        vmem((16, 2 * occ_rows), F32),
        vmem((n, 16, 2 * occ_rows), F32),
        dma((11,)),
        dma((len(struct_spans(planes)),)),
        dma((GROUPS, n)),
        dma((GROUPS, n)),
        dma((GROUPS, levels)),
        dma((GROUPS, levels)),
        dma((GROUPS, n)),
        dma((GROUPS, n)),
        dma((n,)),
        dma((n,)),
    ]
    return pl.pallas_call(
        kernel,
        out_shape=jax.ShapeDtypeStruct(wave.shape, BF16),
        in_specs=[pl.BlockSpec(memory_space=pl.ANY)] * len(operands),
        out_specs=pl.BlockSpec(memory_space=pltpu.VMEM),
        scratch_shapes=scratch,
        compiler_params=pltpu.CompilerParams(
            collective_id=0, has_side_effects=True, vmem_limit_bytes=56 * 2**20
        ),
        name="perturb",
    )(*operands)


def return_kernel(shift, block, out_ref, send_sem, recv_sem):
    pools = lax.axis_size("pool")
    pool = lax.axis_index("pool")
    ahead = lax.rem(pool + shift, pools)
    behind = lax.rem(pool + pools - shift, pools)
    barrier = pltpu.get_barrier_semaphore()
    pl.semaphore_signal(barrier, inc=1, device_id={"pool": ahead}, device_id_type=MESH)
    pl.semaphore_wait(barrier, 1)
    parts = send_sem.shape[0]
    width = block.shape[-1] // parts
    sent = []
    for i in range(parts):
        span = pl.ds(i * width, width)
        copy = pltpu.make_async_remote_copy(
            src_ref=block.at[:, :, :, span],
            dst_ref=out_ref.at[:, :, :, span],
            send_sem=send_sem.at[i],
            recv_sem=recv_sem.at[i],
            device_id={"pool": behind},
            device_id_type=MESH,
        )
        copy.start()
        sent.append(copy)
    for copy in sent:
        copy.wait()


def give_back(shift, parts, block):
    dma = pltpu.SemaphoreType.DMA
    return pl.pallas_call(
        functools.partial(return_kernel, shift),
        out_shape=jax.ShapeDtypeStruct(block.shape, block.dtype),
        in_specs=[pl.BlockSpec(memory_space=pl.ANY)],
        out_specs=pl.BlockSpec(memory_space=pl.ANY),
        scratch_shapes=[dma((parts,)), dma((parts,))],
        compiler_params=pltpu.CompilerParams(
            collective_id=shift.bit_length(), has_side_effects=True
        ),
        name=f"give_back_{shift}",
    )(block)


RETURN_PARTS = 4


def local(
    wave_block,
    occupied,
    radial,
    k_points,
    g_vectors,
    structure,
    positions,
    displacement,
    coupling,
    atom_kind,
    kq_index,
    occ_count,
):
    pools = lax.axis_size("pool")
    n = lax.axis_size("pw")
    operands = (
        wave_block,
        occupied,
        radial,
        k_points.T,
        g_vectors,
        structure,
        positions,
        displacement,
        coupling.transpose(1, 0, 2),
        atom_kind[None, :],
        kq_index[None, :],
        occ_count[None, :],
    )
    block = perturb(operands, pools, n)
    shifts = [1 << level for level in range((pools - 1).bit_length())]
    branch = 31 - lax.clz(kq_index[0])
    runs = [functools.partial(give_back, shift, RETURN_PARTS) for shift in shifts]
    return lax.switch(branch, runs, block)


def solution(mesh):
    return jax.shard_map(
        local,
        mesh=mesh,
        in_specs=(
            P("pool", None, None, "pw"),
            P("pool", None, None, "pw"),
            P("pool", None, "pw"),
            P(),
            P(None, "pw"),
            P(None, None, "pw"),
            P(),
            P(),
            P(),
            P(),
            P(),
            P(),
        ),
        out_specs=P("pool", None, None, "pw"),
        check_vma=False,
    )
```

```python
import functools
import math

import jax
import jax.numpy as jnp
from jax import lax
from jax.experimental import pallas as pl
from jax.experimental.pallas import tpu as pltpu
from jax.sharding import PartitionSpec as P

ATOMS = 216
TYPES = 9
PW = 61440
GROUP = 4
GROUPS = 2
ROWS = 4 * TYPES
PAD = 40
HALF = 128
MESH = pl.DeviceIdType.MESH
F32 = jnp.float32
BF16 = jnp.bfloat16


NEAR = ((2, 1), (1, 1), (3, 1), (2, 0), (0, 1), (1, 0), (3, 0))


def pw_peer(me, n, step, flip):
    return lax.rem(me // 2 + step, n // 2) * 2 + (me % 2 + flip) % 2


def dot_nt(a, b):
    return lax.dot_general(a, b, (((1,), (1,)), ((), ())), preferred_element_type=F32)


def dot_nn(a, b):
    return lax.dot_general(a, b, (((1,), (0,)), ((), ())), preferred_element_type=F32)


def kernel(
    wave_in,
    occ_in,
    radial_in,
    kpts_in,
    gvec_in,
    struct_in,
    pos_in,
    disp_in,
    coupling_in,
    kind_in,
    index_in,
    count_in,
    out_ref,
    wave,
    occ,
    radial,
    kpts,
    gvec,
    struct,
    pos_raw,
    disp_raw,
    coupling,
    kind_raw,
    index,
    count,
    weights,
    moments,
    acc,
    tables,
    kinds,
    couple,
    coef,
    deriv,
    vert,
    vert_full,
    vert_op,
    applied,
    part_send,
    part_recv,
    vert_send,
    candidates,
    gathered,
    corr_send,
    corr_recv,
    load_sem,
    struct_sem,
    part_ssem,
    part_rsem,
    shift_ssem,
    shift_rsem,
    gather_ssem,
    gather_rsem,
    corr_ssem,
    corr_rsem,
):
    pools = lax.axis_size("pool")
    n = lax.axis_size("pw")
    pool = lax.axis_index("pool")
    me = lax.axis_index("pw")
    planes = wave.shape[-1]
    levels = shift_rsem.shape[1]
    halves = (slice(0, HALF), slice(HALF, ATOMS))

    def load(pairs, first):
        copies = []
        for i, (src, dst) in enumerate(pairs):
            copy = pltpu.make_async_copy(src, dst, load_sem.at[first + i])
            copy.start()
            copies.append(copy)
        return copies

    early = load(
        (
            (kpts_in, kpts),
            (radial_in.at[0], radial),
            (gvec_in, gvec),
            (wave_in.at[0], wave),
        ),
        0,
    )
    struct_copies = []
    for i, (start, width) in enumerate(struct_spans(planes)):
        span = pl.ds(start, width)
        copy = pltpu.make_async_copy(
            struct_in.at[:, :, span], struct.at[:, :, span], struct_sem.at[i]
        )
        copy.start()
        struct_copies.append((span, copy))
    late = load(
        (
            (pos_in, pos_raw),
            (disp_in, disp_raw),
            (coupling_in, coupling),
            (kind_in, kind_raw),
            (index_in, index),
            (count_in, count),
        ),
        4,
    )

    barrier = pltpu.get_barrier_semaphore()
    for step, flip in NEAR:
        pl.semaphore_signal(
            barrier, inc=1, device_id={"pw": pw_peer(me, n, step, flip)}, device_id_type=MESH
        )
    for level in reversed(range(levels)):
        sender = lax.rem(pool + pools - (1 << level), pools)
        pl.semaphore_signal(barrier, inc=1, device_id={"pool": sender}, device_id_type=MESH)

    for copy in early:
        copy.wait()
    pool_lane = lax.broadcasted_iota(jnp.int32, (1, pools), 1)

    def pick(values, where):
        return jnp.sum(jnp.where(where, values, jnp.zeros_like(values)), axis=1, keepdims=True)

    here = pick(kpts[...], pool_lane == pool)
    rad = radial[...].astype(F32)
    weights[0:TYPES, :] = rad
    for c in range(3):
        weights[TYPES * (c + 1) : TYPES * (c + 2), :] = rad * (gvec[c : c + 1, :] + here[c : c + 1, :])
    acc[...] = jnp.zeros_like(acc)

    def fill_moments(group, span):
        rows = slice(GROUP * group, GROUP * (group + 1))
        held = jnp.concatenate(
            [wave[0, :, span].astype(F32)[rows], wave[1, :, span].astype(F32)[rows]], 0
        )
        for i in range(ROWS // 2):
            upper = weights[2 * i : 2 * i + 1, span] * held
            lower = weights[2 * i + 1 : 2 * i + 2, span] * held
            moments[group, 16 * i : 16 * i + 16, span] = jnp.concatenate([upper, lower], 0).astype(BF16)

    def send_parts(group):
        for b in range(GROUP):
            for h in range(2):
                re_rows = pl.ds(b, PAD, stride=8)
                im_rows = pl.ds(GROUP + b, PAD, stride=8)
                raw_re = acc[0, h, re_rows, :] + acc[1, h, im_rows, :]
                raw_im = acc[0, h, im_rows, :] - acc[1, h, re_rows, :]
                part_send[group, 2 * b + h] = jnp.concatenate([raw_re, raw_im], 0).astype(BF16)
        sent = []
        for j, (step, flip) in enumerate(NEAR, 1):
            peer = pw_peer(me, n, step, flip)
            copy = pltpu.make_async_remote_copy(
                src_ref=part_send.at[group, peer],
                dst_ref=part_recv.at[group, j],
                send_sem=part_ssem.at[group, j],
                recv_sem=part_rsem.at[group, j],
                device_id={"pw": peer},
                device_id_type=MESH,
            )
            copy.start()
            sent.append(copy)
        return sent

    for span, copy in struct_copies:
        fill_moments(0, span)
        copy.wait()
        for c in range(2):
            product = dot_nt(moments[0, :, span], struct[c, :, span])
            for h, cols in enumerate(halves):
                acc[c, h, 0 : 8 * ROWS, 0 : cols.stop - cols.start] += product[:, cols]
    (occ_copy,) = load(((occ_in.at[0], occ),), 10)
    pl.semaphore_wait(barrier, n - 1 + levels)
    parts = [send_parts(0)]
    fill_moments(1, pl.ds(0, planes))
    for c in range(2):
        product = dot_nt(moments[1], struct[c])
        for h, cols in enumerate(halves):
            acc[c, h, 0 : 8 * ROWS, 0 : cols.stop - cols.start] = product[:, cols]
    parts.append(send_parts(1))

    for copy in late:
        copy.wait()
    half = lax.rem(me, 2)
    lanes = pl.ds(pl.multiple_of(half * HALF, HALF), HALF)
    tables[...] = jnp.zeros_like(tables)
    tables[0:3, 0:ATOMS] = pos_raw[...]
    tables[3:6, 0:ATOMS] = disp_raw[...]
    kinds[...] = jnp.zeros_like(kinds)
    kinds[0:1, 0:ATOMS] = kind_raw[...]
    target = pick(index[...], pool_lane == pool)
    there = pick(kpts[...], pool_lane == target)
    distance = lax.rem(target - pool + pools, pools)

    def phase(point):
        angle = (
            point[0:1, :] * tables[0:1, lanes]
            + point[1:2, :] * tables[1:2, lanes]
            + point[2:3, :] * tables[2:3, lanes]
        )
        return jnp.cos(angle), jnp.sin(angle)

    cos_here, sin_here = phase(here)
    cos_next, sin_next = phase(there)
    disp = [tables[3 + c : 4 + c, lanes] for c in range(3)]
    second = jnp.broadcast_to(kinds[0:1, lanes], (TYPES, HALF)) == 1
    first_table = coupling[:, 0, :]
    second_table = coupling[:, 1, :]
    for u in range(TYPES):
        first_col = jnp.broadcast_to(first_table[:, u : u + 1], (TYPES, HALF))
        second_col = jnp.broadcast_to(second_table[:, u : u + 1], (TYPES, HALF))
        couple[u] = jnp.where(second, second_col, first_col)
    vert[...] = jnp.zeros_like(vert)

    def send_vertex(group):
        total = part_send[group, me].astype(F32)
        for j in reversed(range(1, n)):
            parts[group][j - 1].wait_recv()
            total += part_recv[group, j].astype(F32)
        scale = 1.0 / math.sqrt(PW)
        coef[0] = (cos_here * total[0:PAD] - sin_here * total[PAD:]) * scale
        coef[1] = (cos_here * total[PAD:] + sin_here * total[0:PAD]) * scale

        def moved(part):
            found = None
            for c in range(3):
                term = disp[c] * coef[part, TYPES * (c + 1) : TYPES * (c + 2), :]
                found = term if found is None else found + term
            return found

        deriv[0, 0:TYPES, :] = -moved(1)
        deriv[1, 0:TYPES, :] = moved(0)

        def coupled(source, part):
            found = None
            for u in range(TYPES):
                term = couple[u] * source[part, u : u + 1, :]
                found = term if found is None else found + term
            return found

        zc_re, zc_im = coupled(coef, 0), coupled(coef, 1)
        pieces = [(coupled(deriv, 0), coupled(deriv, 1))]
        pieces += [(disp[c] * zc_im, -disp[c] * zc_re) for c in range(3)]
        shrink = 1.0 / math.sqrt(4 * TYPES * ATOMS)
        for m, (re, im) in enumerate(pieces):
            vert[TYPES * m : TYPES * (m + 1), :] = (cos_next * re + sin_next * im) * shrink
            vert[PAD + TYPES * m : PAD + TYPES * (m + 1), :] = (cos_next * im - sin_next * re) * shrink
        vert_send[group] = vert[...].astype(BF16)
        sent = []
        for level in reversed(range(levels)):
            copy = pltpu.make_async_remote_copy(
                src_ref=vert_send.at[group],
                dst_ref=candidates.at[group, level],
                send_sem=shift_ssem.at[group, level],
                recv_sem=shift_rsem.at[group, level],
                device_id={"pool": lax.rem(pool + (1 << level), pools)},
                device_id_type=MESH,
            )
            copy.start()
            sent.append(copy)
        return sent

    def pass_vertex(group):
        chosen = jnp.zeros((2 * PAD, HALF), F32)
        for level in range(levels):
            chosen = jnp.where(
                distance == (1 << level), candidates[group, level].astype(F32), chosen
            )
        gathered[group, me] = chosen.astype(BF16)
        sent = []
        for j, (step, flip) in enumerate(NEAR, 1):
            copy = pltpu.make_async_remote_copy(
                src_ref=gathered.at[group, me],
                dst_ref=gathered.at[group, me],
                send_sem=gather_ssem.at[group, j],
                recv_sem=gather_rsem.at[group, j],
                device_id={"pw": pw_peer(me, n, step, flip)},
                device_id_type=MESH,
            )
            copy.start()
            sent.append(copy)
        return sent

    def apply_vertex(group):
        for b in range(GROUP):
            for h in range(2):
                piece = gathered[group, 2 * b + h].astype(F32)
                re_rows = pl.ds(b, PAD, stride=8)
                im_rows = pl.ds(GROUP + b, PAD, stride=8)
                vert_full[0, h, re_rows, :] = piece[0:PAD]
                vert_full[0, h, im_rows, :] = piece[PAD:]
                vert_full[1, h, re_rows, :] = -piece[PAD:]
                vert_full[1, h, im_rows, :] = piece[0:PAD]
        for h, cols in enumerate(halves):
            width_of = cols.stop - cols.start
            vert_op[:, :, cols] = vert_full[:, h, 0 : 8 * ROWS, 0:width_of].astype(BF16)
        spread = dot_nn(vert_op[0], struct[0])
        spread += dot_nn(vert_op[1], struct[1])
        total = None
        for i in range(ROWS):
            term = weights[i : i + 1, :] * spread[8 * i : 8 * i + 8]
            total = term if total is None else total + term
        rounded = total.astype(BF16).astype(F32)
        applied[GROUP * group : GROUP * (group + 1), :] = rounded[0:GROUP]
        applied[8 + GROUP * group : 8 + GROUP * (group + 1), :] = rounded[GROUP:]

    shifts = []
    for group in range(GROUPS):
        shifts.append(send_vertex(group))
    passes = []
    for group in range(GROUPS):
        for copy in shifts[group]:
            copy.wait_recv()
        passes.append(pass_vertex(group))
    for sent in parts + shifts:
        for copy in sent:
            copy.wait_send()
    for group in range(GROUPS):
        for copy in passes[group]:
            copy.wait_recv()
        apply_vertex(group)

    occ_copy.wait()
    occ_rows = occ.shape[1]
    corr_send[...] = dot_nt(applied[...].astype(BF16), occ[...].reshape(2 * occ_rows, planes))
    corrs = []
    for j, (step, flip) in enumerate(NEAR, 1):
        copy = pltpu.make_async_remote_copy(
            src_ref=corr_send,
            dst_ref=corr_recv.at[j],
            send_sem=corr_ssem.at[j],
            recv_sem=corr_rsem.at[j],
            device_id={"pw": pw_peer(me, n, step, flip)},
            device_id_type=MESH,
        )
        copy.start()
        corrs.append(copy)
    live = pick(count[...], pool_lane == pool)
    for sent in passes:
        for copy in sent:
            copy.wait_send()
    total = corr_send[...]
    for j in reversed(range(1, n)):
        corrs[j - 1].wait_recv()
        total += corr_recv[j]
    row = lax.broadcasted_iota(jnp.int32, total.shape, 0)
    lane = lax.broadcasted_iota(jnp.int32, total.shape, 1)
    swapped = pltpu.roll(jnp.concatenate([total[8:], total[:8]], 0), occ_rows, 1)
    same = (row >= 8) == (lane >= occ_rows)
    combined = jnp.where(same, total + swapped, total - swapped)
    state = jnp.where(lane >= occ_rows, lane - occ_rows, lane)
    kept = jnp.where(state < live, combined, 0.0).astype(BF16)
    removed = dot_nn(kept, occ[...].reshape(2 * occ_rows, planes))
    response = (applied[...] - removed).astype(BF16)
    out_ref[0, 0] = response[:8]
    out_ref[0, 1] = response[8:]
    for copy in corrs:
        copy.wait_send()


def struct_spans(planes):
    unit = planes // 20
    return ((0, 4 * unit), (4 * unit, 6 * unit), (10 * unit, 10 * unit))


def perturb(operands, pools, n):
    wave, occ = operands[0], operands[1]
    planes = wave.shape[-1]
    occ_rows = occ.shape[2]
    levels = (pools - 1).bit_length()
    vmem, dma = pltpu.VMEM, pltpu.SemaphoreType.DMA
    scratch = [
        vmem((2, 8, planes), BF16),
        vmem((2, occ_rows, planes), BF16),
        vmem((TYPES, planes), BF16),
        vmem((3, pools), F32),
        vmem((3, planes), F32),
        vmem((2, ATOMS, planes), BF16),
        vmem((3, ATOMS), F32),
        vmem((3, ATOMS), F32),
        vmem((TYPES, 2, TYPES), F32),
        vmem((1, ATOMS), jnp.int32),
        vmem((1, pools), jnp.int32),
        vmem((1, pools), jnp.int32),
        vmem((PAD, planes), F32),
        vmem((GROUPS, 8 * ROWS, planes), BF16),
        vmem((2, 2, 8 * PAD, HALF), F32),
        vmem((8, 2 * HALF), F32),
        vmem((8, 2 * HALF), jnp.int32),
        vmem((TYPES, TYPES, HALF), F32),
        vmem((2, PAD, HALF), F32),
        vmem((2, 16, HALF), F32),
        vmem((2 * PAD, HALF), F32),
        vmem((2, 2, 8 * PAD, HALF), F32),
        vmem((2, 8 * ROWS, ATOMS), BF16),
        vmem((16, planes), F32),
        vmem((GROUPS, n, 2 * PAD, HALF), BF16),
        vmem((GROUPS, n, 2 * PAD, HALF), BF16),
        vmem((GROUPS, 2 * PAD, HALF), BF16),
        vmem((GROUPS, levels, 2 * PAD, HALF), BF16),
        vmem((GROUPS, n, 2 * PAD, HALF), BF16),
        vmem((16, 2 * occ_rows), F32),
        vmem((n, 16, 2 * occ_rows), F32),
        dma((11,)),
        dma((len(struct_spans(planes)),)),
        dma((GROUPS, n)),
        dma((GROUPS, n)),
        dma((GROUPS, levels)),
        dma((GROUPS, levels)),
        dma((GROUPS, n)),
        dma((GROUPS, n)),
        dma((n,)),
        dma((n,)),
    ]
    return pl.pallas_call(
        kernel,
        out_shape=jax.ShapeDtypeStruct(wave.shape, BF16),
        in_specs=[pl.BlockSpec(memory_space=pl.ANY)] * len(operands),
        out_specs=pl.BlockSpec(memory_space=pltpu.VMEM),
        scratch_shapes=scratch,
        compiler_params=pltpu.CompilerParams(
            collective_id=0, has_side_effects=True, vmem_limit_bytes=56 * 2**20
        ),
        name="perturb",
    )(*operands)


def return_kernel(shift, block, out_ref, send_sem, recv_sem):
    pools = lax.axis_size("pool")
    pool = lax.axis_index("pool")
    ahead = lax.rem(pool + shift, pools)
    behind = lax.rem(pool + pools - shift, pools)
    barrier = pltpu.get_barrier_semaphore()
    pl.semaphore_signal(barrier, inc=1, device_id={"pool": ahead}, device_id_type=MESH)
    pl.semaphore_wait(barrier, 1)
    parts = send_sem.shape[0]
    width = block.shape[-1] // parts
    sent = []
    for i in range(parts):
        span = pl.ds(i * width, width)
        copy = pltpu.make_async_remote_copy(
            src_ref=block.at[:, :, :, span],
            dst_ref=out_ref.at[:, :, :, span],
            send_sem=send_sem.at[i],
            recv_sem=recv_sem.at[i],
            device_id={"pool": behind},
            device_id_type=MESH,
        )
        copy.start()
        sent.append(copy)
    for copy in sent:
        copy.wait()


def give_back(shift, parts, block):
    dma = pltpu.SemaphoreType.DMA
    return pl.pallas_call(
        functools.partial(return_kernel, shift),
        out_shape=jax.ShapeDtypeStruct(block.shape, block.dtype),
        in_specs=[pl.BlockSpec(memory_space=pl.ANY)],
        out_specs=pl.BlockSpec(memory_space=pl.ANY),
        scratch_shapes=[dma((parts,)), dma((parts,))],
        compiler_params=pltpu.CompilerParams(
            collective_id=shift.bit_length(), has_side_effects=True
        ),
        name=f"give_back_{shift}",
    )(block)


RETURN_PARTS = 4


def local(
    wave_block,
    occupied,
    radial,
    k_points,
    g_vectors,
    structure,
    positions,
    displacement,
    coupling,
    atom_kind,
    kq_index,
    occ_count,
):
    pools = lax.axis_size("pool")
    n = lax.axis_size("pw")
    operands = (
        wave_block,
        occupied,
        radial,
        k_points.T,
        g_vectors,
        structure,
        positions,
        displacement,
        coupling.transpose(1, 0, 2),
        atom_kind[None, :],
        kq_index[None, :],
        occ_count[None, :],
    )
    block = perturb(operands, pools, n)
    shifts = [1 << level for level in range((pools - 1).bit_length())]
    branch = 31 - lax.clz(kq_index[0])
    runs = [functools.partial(give_back, shift, RETURN_PARTS) for shift in shifts]
    return lax.switch(branch, runs, block)


def solution(mesh):
    return jax.shard_map(
        local,
        mesh=mesh,
        in_specs=(
            P("pool", None, None, "pw"),
            P("pool", None, None, "pw"),
            P("pool", None, "pw"),
            P(),
            P(None, "pw"),
            P(None, None, "pw"),
            P(),
            P(),
            P(),
            P(),
            P(),
            P(),
        ),
        out_specs=P("pool", None, None, "pw"),
        check_vma=False,
    )
```
